32 devices in a mesh: dp: 2 (over core), seq: 8 (over z, y), tensor: 2 (over x).
Axes of the slice: x: 2, y: 2, z: 4, core: 2. Of those that a mesh axis runs over, the one named last changes fastest.
Arguments:
- queries: bfloat16 [4096, 2048], P(('dp', 'seq'), 'tensor'), parts along dimension 0
- routed_key_rows: bfloat16 [4096, 512], P(('dp', 'seq'), 'tensor'), parts along dimension 0
- routed_value_rows: bfloat16 [4096, 512], P(('dp', 'seq'), 'tensor'), parts along dimension 0, may hold values from -6 to 6
- grad_out: bfloat16 [4096, 2048], P(('dp', 'seq'), 'tensor'), parts along dimension 0, may hold values from -6 to 6
- gate_logit: float32 [4096], P(('dp', 'seq')), parts along dimension 0, may hold values from -6 to 6
- block_ids: int32 [16, 2], P('dp'), parts along dimension 0, may hold values from 0 to 15, as said below
- block_counts: int32 [16], P('dp'), parts along dimension 0, may hold values from 1 to 2, as said below
Outputs:
- query_grads: bfloat16 [4096, 2048], P(('dp', 'seq'), 'tensor'), parts along dimension 0
- key_grads: bfloat16 [4096, 512], P(('dp', 'seq'), 'tensor'), parts along dimension 0
- value_grads: bfloat16 [4096, 512], P(('dp', 'seq'), 'tensor'), parts along dimension 0
- gate_grads: float32 [4096], P(('dp', 'seq')), parts along dimension 0
The draws below stay inside these ranges and needn't reach their ends.
There are 2 independent parts, one for each index of `dp`. The reference program is written for one: setup_inputs(seed, part) draws one part's arguments, and reference() takes and returns one part's arrays. A program takes and returns all parts, laid end to end along the dimension named above; each array names one. Nothing has to cross between parts.
Inputs may be any that keep to these rules, and one draw needn't show every extreme that they name: `block_ids`: within each shard the routed block positions are distinct. Only the first block_counts[s] slots of shard s hold routed blocks; the rows of the other slots are not live.
All inputs are finite; a program needn't handle non-finite values.
Results may differ from the reference program's by a relative error of at most 0.028.
Values may be sent and summed in bfloat16 or wider, within the bound.
A program may use at most 128 MiB of HBM per device.

```python
import jax
import jax.numpy as jnp
from jax import lax

HEAD_SIZE = 128
QUERY_HEADS = 16
KEY_VALUE_HEADS = 4
BLK = 128
CAP = 2
SPAN_BLK = 16
SHARD_ROWS = 256
ROUTED_ROWS = 2048
N_SEQ = 8


def base_keys(key):
    unscaled_keys = jnp.clip(jax.random.normal(jax.random.fold_in(key, 11), (ROUTED_ROWS, KEY_VALUE_HEADS * HEAD_SIZE), jnp.float32), -4.0, 4.0)
    row_index = jnp.arange(ROUTED_ROWS)
    slot_row = row_index % (CAP * BLK)
    marked = slot_row == BLK // 2
    before = slot_row == BLK // 2 - 1
    lifted = jnp.where(marked[:, None], unscaled_keys, unscaled_keys)
    return jnp.where(before[:, None], unscaled_keys, lifted)


def draw_routed_key_rows(key, part):
    shaped = base_keys(key)
    return shaped.astype(jnp.bfloat16)


def draw_queries(key, part):
    key = jax.random.fold_in(key, 3)
    drawn = jnp.clip(jax.random.normal(jax.random.fold_in(key, 1), (ROUTED_ROWS, QUERY_HEADS * HEAD_SIZE), jnp.float32), -6.0, 6.0)
    return drawn.astype(jnp.bfloat16)


def place_block(perm_row, wanted, slot_at):
    slot_index = jnp.arange(SPAN_BLK)
    held = perm_row[slot_at]
    return jnp.where(perm_row == wanted, held, jnp.where(slot_index == slot_at, wanted, perm_row))


def draw_block_ids(key, part):
    key = jax.random.fold_in(key, 7)
    shard_keys = jax.random.split(jax.random.fold_in(key, 1), N_SEQ)
    perms = jax.vmap(lambda shard_key: jax.random.permutation(shard_key, SPAN_BLK))(shard_keys).astype(jnp.int32)
    top_at = jax.random.randint(jax.random.fold_in(key, 2), (), 0, N_SEQ)
    low_at = (top_at + 1 + jax.random.randint(jax.random.fold_in(key, 3), (), 0, N_SEQ - 1)) % N_SEQ
    shard_index = jnp.arange(N_SEQ)[:, None]
    top_rows = jax.vmap(lambda row: place_block(row, SPAN_BLK - 1, 0))(perms)
    perms = jnp.where(shard_index == top_at, top_rows, perms)
    low_rows = jax.vmap(lambda row: place_block(row, 0, CAP - 1))(perms)
    perms = jnp.where(shard_index == low_at, low_rows, perms)
    return perms[:, :CAP].astype(jnp.int32)


def draw_block_counts(key, part):
    key = jax.random.fold_in(key, 5)
    counts = jax.random.randint(jax.random.fold_in(key, 1), (N_SEQ,), 1, CAP + 1)
    full_at = jax.random.randint(jax.random.fold_in(key, 2), (), 0, N_SEQ)
    low_at = (full_at + 1 + jax.random.randint(jax.random.fold_in(key, 3), (), 0, N_SEQ - 1)) % N_SEQ
    shard_index = jnp.arange(N_SEQ)
    counts = jnp.where(shard_index == full_at, CAP, jnp.where(shard_index == low_at, 1, counts))
    return counts.astype(jnp.int32)


def levels(stream_key, extent, pieces, least, high):
    def one(dim, shards_of):
        steps = jax.random.uniform(jax.random.fold_in(jax.random.fold_in(stream_key, 6), dim), (shards_of,), jnp.float32, least / len(pieces), high / len(pieces))
        return jnp.repeat(jnp.exp(steps), extent[dim] // shards_of).reshape((-1,) + (1,) * (len(extent) - dim - 1))

    loudness = one(*pieces[0])
    for cut in pieces[1:]:
        loudness = loudness * one(*cut)
    return loudness


def noise(key, extent, deviation, bound, pieces=(), held_as=jnp.bfloat16):
    factor_of = levels(key, extent, pieces, -0.22, 0.18) if pieces else 1.0
    entries = jax.random.normal(key, extent, jnp.float32) * deviation * factor_of
    return jnp.minimum(jnp.maximum(entries, -bound), bound).astype(held_as)


def setup_inputs(seed: int = 0, part: int = 0) -> dict:
    arg_keys = jax.random.split(jax.random.key(seed), 8)
    own_keys = jax.random.split(jax.random.fold_in(arg_keys[7], part), 8)
    queries = draw_queries(jax.random.fold_in(jax.random.fold_in(arg_keys[7], part), 71), part)
    routed_key_rows = draw_routed_key_rows(jax.random.fold_in(jax.random.fold_in(arg_keys[7], part), 71), part)
    routed_value_rows = noise(own_keys[2], (ROUTED_ROWS, KEY_VALUE_HEADS * HEAD_SIZE), 1.0, 6.0, ((0, 8), (1, 2)))
    grad_out = noise(own_keys[3], (ROUTED_ROWS, QUERY_HEADS * HEAD_SIZE), 1.0, 6.0, ((0, 8), (1, 2)))
    gate_logit = noise(own_keys[4], (ROUTED_ROWS,), 2.0, 6.0, ((0, 8),), jnp.float32)
    block_ids = draw_block_ids(jax.random.fold_in(jax.random.fold_in(arg_keys[7], part), 71), part)
    block_counts = draw_block_counts(jax.random.fold_in(jax.random.fold_in(arg_keys[7], part), 71), part)
    return {"queries": queries, "routed_key_rows": routed_key_rows, "routed_value_rows": routed_value_rows, "grad_out": grad_out, "gate_logit": gate_logit, "block_ids": block_ids, "block_counts": block_counts}


def token_positions(block_ids, block_counts):
    shard_count, slot_count = block_ids.shape
    shard_index = jnp.arange(shard_count, dtype=jnp.int32)[:, None]
    block_start = (shard_index * SPAN_BLK + block_ids.astype(jnp.int32)) * BLK
    offsets = jnp.arange(BLK, dtype=jnp.int32)
    positions = (block_start[:, :, None] + offsets[None, None, :]).reshape(-1)
    slot_live = jnp.arange(slot_count, dtype=jnp.int32)[None, :] < block_counts.astype(jnp.int32)[:, None]
    live_rows = jnp.broadcast_to(slot_live[:, :, None], (shard_count, slot_count, BLK)).reshape(-1)
    return positions, live_rows


def low_round(values_in):
    return lax.optimization_barrier(values_in.astype(jnp.bfloat16)).astype(jnp.float32)


def reference(queries, routed_key_rows, routed_value_rows, grad_out, gate_logit, block_ids, block_counts):
    positions, live_rows = token_positions(block_ids, block_counts)
    query_group_width = QUERY_HEADS // KEY_VALUE_HEADS
    score_scale = HEAD_SIZE ** -0.5
    gate_value = jax.nn.sigmoid(gate_logit.astype(jnp.float32))
    output_gradients = (gate_value[:, None] * grad_out.astype(jnp.float32)).astype(jnp.bfloat16)
    heads_of_keys = routed_key_rows.astype(jnp.float32).reshape(ROUTED_ROWS, KEY_VALUE_HEADS, HEAD_SIZE)
    heads_of_values = routed_value_rows.astype(jnp.float32).reshape(ROUTED_ROWS, KEY_VALUE_HEADS, HEAD_SIZE)
    query_complete = queries.astype(jnp.float32).reshape(N_SEQ, SHARD_ROWS, KEY_VALUE_HEADS, query_group_width, HEAD_SIZE)
    output_gradient_full = output_gradients.astype(jnp.float32).reshape(N_SEQ, SHARD_ROWS, KEY_VALUE_HEADS, query_group_width, HEAD_SIZE)
    key_index = jnp.arange(ROUTED_ROWS, dtype=jnp.int32)
    query_index = key_index.reshape(N_SEQ, SHARD_ROWS)
    pos_rows = positions.reshape(N_SEQ, SHARD_ROWS)
    live_query = live_rows.reshape(N_SEQ, SHARD_ROWS)

    def shard_step(state_now, inputs):
        key_sum, value_sum = state_now
        heads_of_queries, output_gradient_heads, query_pos, query_live, query_rows = inputs
        scores = jnp.einsum('rkgd,jkd->kgrj', heads_of_queries, heads_of_keys) * score_scale
        allowed = (live_rows[None, :] & (positions[None, :] <= query_pos[:, None])) | (key_index[None, :] == query_rows[:, None])
        row_max = jnp.max(jnp.where(allowed, scores, -jnp.inf), axis=-1, keepdims=True)
        weights = jnp.where(allowed, jnp.exp(scores - row_max), 0.0)
        probabilities = weights / jnp.sum(weights, axis=-1, keepdims=True) * query_live.astype(jnp.float32)[:, None]
        prob_grads = jnp.einsum('rkgd,jkd->kgrj', output_gradient_heads, heads_of_values)
        delta_rows = jnp.sum(probabilities * prob_grads, axis=-1)
        score_gradients = low_round(probabilities * (prob_grads - delta_rows[..., None]) * score_scale)
        probability_reduced = low_round(probabilities)
        query_grad = jnp.einsum('kgrj,jkd->rkgd', score_gradients, heads_of_keys).reshape(SHARD_ROWS, QUERY_HEADS * HEAD_SIZE).astype(jnp.bfloat16)
        key_portion = jnp.einsum('fimw,mfiy->wfy', score_gradients, heads_of_queries).reshape(ROUTED_ROWS, KEY_VALUE_HEADS * HEAD_SIZE)
        value_portion = jnp.einsum('fimw,mfiy->wfy', probability_reduced, output_gradient_heads).reshape(ROUTED_ROWS, KEY_VALUE_HEADS * HEAD_SIZE)
        key_sum = key_sum + low_round(key_portion)
        value_sum = value_sum + low_round(value_portion)
        return (key_sum, value_sum), (query_grad, jnp.sum(delta_rows, axis=(0, 1)))

    empty_sum_matrix = jnp.zeros((ROUTED_ROWS, KEY_VALUE_HEADS * HEAD_SIZE), jnp.float32)
    (key_sum, value_sum), (query_grads, delta_sums) = lax.scan(
        shard_step, (empty_sum_matrix, empty_sum_matrix), (query_complete, output_gradient_full, pos_rows, live_query, query_index))
    gate_grads = (1.0 - gate_value) * delta_sums.reshape(ROUTED_ROWS)
    return (query_grads.reshape(ROUTED_ROWS, QUERY_HEADS * HEAD_SIZE), key_sum.astype(jnp.bfloat16),
            value_sum.astype(jnp.bfloat16), gate_grads)
```

```python
import functools
import math

import jax
import jax.numpy as jnp
from jax import lax
from jax.experimental import pallas as pl
from jax.experimental.pallas import tpu as pltpu
from jax.sharding import PartitionSpec as P

D = 128
GROUP = 4
BLK = 128
SCALE = D ** -0.5
EXP2_SCALE = SCALE * math.log2(math.e)
MESH = pl.DeviceIdType.MESH
F32 = jnp.float32
BF16 = jnp.bfloat16


def mm(a, b):
    return jnp.dot(a, b, preferred_element_type=F32)


def kernel(
    n, kv_heads,
    ids_ref, counts_ref, q_ref, k_ref, v_ref, go_ref, gate_ref,
    dq_ref, dk_ref, dv_ref, dgate_ref,
    kv, qn, qt, on, ot, exps, block_max, row_max, row_sum, row_dot, delta, factor,
    dqt, own, bias, ysend, yrecv, zsend, zrecv, tsend, trecv,
    kv_sem, up_sem, across_sem, ysend_sem, yrecv_sem, zsend_sem, zrecv_sem, t_sem,
):
    rows = q_ref.shape[0]
    me = lax.axis_index("seq")
    tensor = lax.axis_index("tensor")
    half = n // 2
    z, y = me // 2, me % 2
    partner = 2 * z + (1 - y)

    def up_copy(g, zd):
        return pltpu.make_async_remote_copy(
            kv.at[g, me], kv.at[g, me], up_sem.at[g, zd], kv_sem.at[g, me],
            device_id={"seq": 2 * zd + y}, device_id_type=MESH)

    def across_copy(g, zz):
        b = 2 * zz + y
        return pltpu.make_async_remote_copy(
            kv.at[g, b], kv.at[g, b], across_sem.at[g, zz], kv_sem.at[g, b],
            device_id={"seq": partner}, device_id_type=MESH)

    def arrived(g, b):
        pltpu.make_async_remote_copy(
            kv.at[g, b], kv.at[g, b], up_sem.at[g, 0], kv_sem.at[g, b],
            device_id={"seq": partner}, device_id_type=MESH).wait_recv()

    def ygrad_copy(g, zz):
        return pltpu.make_async_remote_copy(
            ysend.at[g, zz], yrecv.at[g, zz], ysend_sem.at[g, zz], yrecv_sem.at[g, zz],
            device_id={"seq": partner}, device_id_type=MESH)

    def zgrad_copy(g, zz):
        return pltpu.make_async_remote_copy(
            zsend.at[g, zz], zrecv.at[g, z], zsend_sem.at[g, zz], zrecv_sem.at[g, z],
            device_id={"seq": 2 * zz + y}, device_id_type=MESH)

    def zgrad_arrived(g, zs):
        pltpu.make_async_remote_copy(
            zsend.at[g, zs], zrecv.at[g, zs], zsend_sem.at[g, zs], zrecv_sem.at[g, zs],
            device_id={"seq": partner}, device_id_type=MESH).wait_recv()

    def tensor_copy():
        return pltpu.make_async_remote_copy(
            tsend, trecv, t_sem.at[0], t_sem.at[1],
            device_id={"tensor": 1 - tensor}, device_id_type=MESH)

    def loop(lo, hi, body):
        def step(i, carry):
            body(i)
            return carry
        lax.fori_loop(lo, hi, step, 0)

    barrier = pltpu.get_barrier_semaphore()
    pl.semaphore_signal(barrier, inc=1, device_id={"seq": partner}, device_id_type=MESH)
    pl.semaphore_signal(barrier, inc=1, device_id={"tensor": 1 - tensor}, device_id_type=MESH)

    def greet(step):
        other = lax.rem(z + step, half)
        pl.semaphore_signal(barrier, inc=1, device_id={"seq": 2 * other + y}, device_id_type=MESH)
    loop(1, half, greet)

    for g in range(kv_heads):
        kv[g, me, 0] = k_ref[:, g * D:(g + 1) * D]
        kv[g, me, 1] = v_ref[:, g * D:(g + 1) * D]
    pl.semaphore_wait(barrier, half + 1)

    def send_own(g):
        @pl.when(y == 0)
        def _():
            across_copy(g, z).start()
        loop(z + 1, half, lambda zd: up_copy(g, zd).start())

    send_own(0)

    gate = 1.0 / (1.0 + jnp.exp(-gate_ref[...]))
    gate_columns = jnp.transpose(jnp.broadcast_to(gate, (D, rows)))
    for g in range(kv_heads):
        for h in range(GROUP):
            source = slice((g * GROUP + h) * D, (g * GROUP + h + 1) * D)
            at = slice(h * rows, (h + 1) * rows)
            out_grad = (gate_columns * go_ref[:, source].astype(F32)).astype(BF16)
            on[g, at, :] = out_grad
            ot[g, :, at] = jnp.transpose(out_grad)
            qn[g, at, :] = q_ref[:, source]
            qt[g, :, at] = jnp.transpose(q_ref[:, source])

    def by_slot(index, first, second):
        return jnp.where(index < BLK, first, second)

    key_row = lax.broadcasted_iota(jnp.int32, (rows, rows), 0)
    query_row = lax.broadcasted_iota(jnp.int32, (rows, rows), 1)
    id0, id1, count = ids_ref[me, 0], ids_ref[me, 1], counts_ref[me]
    key_pos = by_slot(key_row, id0 * BLK, id1 * BLK - BLK) + key_row
    query_pos = by_slot(query_row, id0 * BLK, id1 * BLK - BLK) + query_row
    key_slot = by_slot(key_row, 0, 1)
    allowed = ((key_slot < count) & (key_pos <= query_pos)) | (key_row == query_row)
    bias[...] = jnp.where(allowed, 0.0, -jnp.inf).astype(F32)
    query_slot = by_slot(lax.broadcasted_iota(jnp.int32, (1, rows), 1), 0, 1)
    live = jnp.where(query_slot < count, 1.0, 0.0).astype(F32)

    def first_pass(g, b, is_own):
        keys, values = kv[g, b, 0], kv[g, b, 1]
        shut0 = jnp.where(counts_ref[b] > 0, 0.0, -jnp.inf).astype(F32)
        shut1 = jnp.where(counts_ref[b] > 1, 0.0, -jnp.inf).astype(F32)
        for h in range(GROUP):
            at = slice(h * rows, (h + 1) * rows)
            s = mm(keys, qt[g, :, at])
            if is_own:
                s = s + bias[...]
            else:
                s = jnp.concatenate([s[:BLK] + shut0, s[BLK:] + shut1], axis=0)
            prob_grads = mm(values, ot[g, :, at])
            top = jnp.max(s, axis=0, keepdims=True)
            if not is_own:
                before = row_max[:, at]
                top = jnp.maximum(before, top)
            e = jnp.exp2((s - top) * EXP2_SCALE)
            total = jnp.sum(e, axis=0, keepdims=True)
            dot = jnp.sum(e * prob_grads, axis=0, keepdims=True)
            if not is_own:
                shrink = jnp.exp2((before - top) * EXP2_SCALE)
                total = total + row_sum[:, at] * shrink
                dot = dot + row_dot[:, at] * shrink
            row_max[:, at] = top
            row_sum[:, at] = total
            row_dot[:, at] = dot
            block_max[b, :, at] = top
            exps[b, :, at] = e.astype(BF16)

    def gather(g):
        first_pass(g, me, True)

        @pl.when(y == 1)
        def _():
            arrived(g, partner)
            first_pass(g, partner, False)

        def step(k):
            zz = z - k
            same, other = 2 * zz + y, 2 * zz + 1 - y
            arrived(g, same)
            across_copy(g, zz).start()
            first_pass(g, same, False)
            arrived(g, other)
            first_pass(g, other, False)
        loop(1, z + 1, step)

    def close_stats(g):
        for h in range(GROUP):
            at = slice(h * rows, (h + 1) * rows)
            inverse = live / row_sum[:, at]
            delta[:, at] = row_dot[:, at] * inverse
            factor[:, at] = inverse
        dqt[...] = jnp.zeros_like(dqt)

    def second_pass(g, b):
        keys, values = kv[g, b, 0], kv[g, b, 1]
        keys_t = jnp.transpose(keys)
        dk = jnp.zeros((rows, D), F32)
        dv = jnp.zeros((rows, D), F32)
        for h in range(GROUP):
            at = slice(h * rows, (h + 1) * rows)
            weight = jnp.exp2((block_max[b, :, at] - row_max[:, at]) * EXP2_SCALE) * factor[:, at]
            probs = exps[b, :, at].astype(F32) * weight
            prob_grads = mm(values, ot[g, :, at])
            score_grads = (probs * (prob_grads - delta[:, at])).astype(BF16)
            dv = dv + mm(probs.astype(BF16), on[g, at, :])
            dk = dk + mm(score_grads, qn[g, at, :])
            dqt[:, at] += mm(keys_t, score_grads)
        return dk * SCALE, dv

    def grads(g):
        def to_partner(zz):
            dk, dv = second_pass(g, 2 * zz + 1 - y)
            ysend[g, zz, 0] = dk.astype(BF16)
            ysend[g, zz, 1] = dv.astype(BF16)
            ygrad_copy(g, zz).start()

        def keep(zz):
            dk, dv = second_pass(g, 2 * zz + y)
            own[g, zz, 0] = dk
            own[g, zz, 1] = dv

        loop(0, z + y, to_partner)
        loop(0, z + 1, keep)
        for h in range(GROUP):
            at = slice(h * rows, (h + 1) * rows)
            target = slice((g * GROUP + h) * D, (g * GROUP + h + 1) * D)
            dq_ref[:, target] = jnp.transpose(dqt[:, at] * SCALE).astype(BF16)

    def to_owners(g):
        def step(zz):
            ygrad_copy(g, zz).wait_recv()
            zsend[g, zz] = (own[g, zz] + yrecv[g, zz].astype(F32)).astype(BF16)
            zgrad_copy(g, zz).start()
        loop(0, z, step)

    def finish(g):
        @pl.when(y == 0)
        def _():
            ygrad_copy(g, z).wait_recv()
            own[g, z] = own[g, z] + yrecv[g, z].astype(F32)

        def step(zs):
            zgrad_arrived(g, zs)
            own[g, z] = own[g, z] + zrecv[g, zs].astype(F32)
        loop(z + 1, half, step)
        dk_ref[:, g * D:(g + 1) * D] = own[g, z, 0].astype(BF16)
        dv_ref[:, g * D:(g + 1) * D] = own[g, z, 1].astype(BF16)

    delta_sum = jnp.zeros((1, rows), F32)
    for g in range(kv_heads):
        gather(g)
        if g + 1 < kv_heads:
            send_own(g + 1)
        close_stats(g)
        for h in range(GROUP):
            delta_sum = delta_sum + delta[:, h * rows:(h + 1) * rows]
        if g + 1 == kv_heads:
            tsend[...] = jnp.broadcast_to(delta_sum, tsend.shape)
            tensor_copy().start()
        if g > 0:
            to_owners(g - 1)
        grads(g)
    to_owners(kv_heads - 1)
    tensor_copy().wait_recv()
    dgate_ref[...] = (1.0 - gate) * (delta_sum + trecv[0:1, :])
    for g in range(kv_heads):
        finish(g)

    tensor_copy().wait_send()
    for g in range(kv_heads):
        loop(z + 1, half, lambda zd: up_copy(g, zd).wait_send())
        loop(0, z + 1 - y, lambda zz: across_copy(g, zz).wait_send())
        loop(0, z + y, lambda zz: ygrad_copy(g, zz).wait_send())
        loop(0, z, lambda zz: zgrad_copy(g, zz).wait_send())


def local(n, queries, keys, values, grad_out, gate_logit, block_ids, block_counts):
    rows, width = queries.shape
    kv_width = keys.shape[1]
    kv_heads = kv_width // D
    half = n // 2
    group_rows = GROUP * rows
    vmem = pl.BlockSpec(memory_space=pltpu.VMEM)
    smem = pl.BlockSpec(memory_space=pltpu.SMEM)
    pair = (2, rows, D)
    sem = pltpu.SemaphoreType.DMA
    dq, dk, dv, dgate = pl.pallas_call(
        functools.partial(kernel, n, kv_heads),
        out_shape=(
            jax.ShapeDtypeStruct((rows, width), BF16),
            jax.ShapeDtypeStruct((rows, kv_width), BF16),
            jax.ShapeDtypeStruct((rows, kv_width), BF16),
            jax.ShapeDtypeStruct((1, rows), F32),
        ),
        in_specs=[smem, smem, vmem, vmem, vmem, vmem, vmem],
        out_specs=(vmem, vmem, vmem, vmem),
        scratch_shapes=[
            pltpu.VMEM((kv_heads, n) + pair, BF16),
            pltpu.VMEM((kv_heads, group_rows, D), BF16),
            pltpu.VMEM((kv_heads, D, group_rows), BF16),
            pltpu.VMEM((kv_heads, group_rows, D), BF16),
            pltpu.VMEM((kv_heads, D, group_rows), BF16),
            pltpu.VMEM((n, rows, group_rows), BF16),
            pltpu.VMEM((n, 1, group_rows), F32),
            pltpu.VMEM((1, group_rows), F32),
            pltpu.VMEM((1, group_rows), F32),
            pltpu.VMEM((1, group_rows), F32),
            pltpu.VMEM((1, group_rows), F32),
            pltpu.VMEM((1, group_rows), F32),
            pltpu.VMEM((D, group_rows), F32),
            pltpu.VMEM((kv_heads, half) + pair, F32),
            pltpu.VMEM((rows, rows), F32),
            pltpu.VMEM((kv_heads, half) + pair, BF16),
            pltpu.VMEM((kv_heads, half) + pair, BF16),
            pltpu.VMEM((kv_heads, half) + pair, BF16),
            pltpu.VMEM((kv_heads, half) + pair, BF16),
            pltpu.VMEM((8, rows), F32),
            pltpu.VMEM((8, rows), F32),
            sem((kv_heads, n)),
            sem((kv_heads, half)),
            sem((kv_heads, half)),
            sem((kv_heads, half)),
            sem((kv_heads, half)),
            sem((kv_heads, half)),
            sem((kv_heads, half)),
            sem((2,)),
        ],
        compiler_params=pltpu.CompilerParams(
            collective_id=0, has_side_effects=True, vmem_limit_bytes=60 * 1024 * 1024
        ),
        cost_estimate=pl.CostEstimate(
            flops=12 * n * rows * rows * width,
            bytes_accessed=6 * rows * (width + kv_width),
            transcendentals=n * rows * rows * width // D,
        ),
        name="mod_attention_grads",
    )(block_ids, block_counts, queries, keys, values, grad_out, gate_logit.reshape(1, rows))
    return dq, dk, dv, dgate.reshape(rows)


def solution(mesh):
    in_specs = (
        P(("dp", "seq"), "tensor"),
        P(("dp", "seq"), "tensor"),
        P(("dp", "seq"), "tensor"),
        P(("dp", "seq"), "tensor"),
        P(("dp", "seq")),
        P("dp", None),
        P("dp"),
    )
    out_specs = (
        P(("dp", "seq"), "tensor"),
        P(("dp", "seq"), "tensor"),
        P(("dp", "seq"), "tensor"),
        P(("dp", "seq")),
    )
    return jax.shard_map(
        functools.partial(local, mesh.shape["seq"]),
        mesh=mesh, in_specs=in_specs, out_specs=out_specs, check_vma=False,
    )
```

```python
import functools
import math

import jax
import jax.numpy as jnp
from jax import lax
from jax.experimental import pallas as pl
from jax.experimental.pallas import tpu as pltpu
from jax.sharding import PartitionSpec as P

D = 128
GROUP = 4
BLK = 128
SCALE = D ** -0.5
EXP2_SCALE = SCALE * math.log2(math.e)
MESH = pl.DeviceIdType.MESH
F32 = jnp.float32
BF16 = jnp.bfloat16


def mm(a, b):
    return jnp.dot(a, b, preferred_element_type=F32)


def kernel(
    n,
    ids_ref, counts_ref, q_ref, k_ref, v_ref, go_ref, gate_ref,
    dq_ref, dk_ref, dv_ref, dgate_ref,
    kv, kvx, qx, ox, qn, qt, on, ot, exps, block_max, row_max, row_sum, row_dot, delta, factor,
    dqt, own, bias, low, scored, zsend, zrecv, dqx, dqr, dkvx, dkvr, tsend, trecv,
    kv_sem, up_sem, zsend_sem, zrecv_sem, y_send_sem, y_recv_sem, t_sem,
):
    rows = q_ref.shape[0]
    wide = GROUP * rows
    me = lax.axis_index("seq")
    tensor = lax.axis_index("tensor")
    half = n // 2
    z, y = me // 2, me % 2
    partner = 2 * z + (1 - y)

    def remote(source, target, send_sem, recv_sem, seq):
        return pltpu.make_async_remote_copy(
            source, target, send_sem, recv_sem, device_id={"seq": seq}, device_id_type=MESH)

    def part(p):
        return pl.ds(pl.multiple_of(p * wide, wide), wide)

    def lanes(p, h):
        return pl.ds(pl.multiple_of(p * wide + h * rows, rows), rows)

    def y_copy(i):
        source, target = (
            (kvx, kv.at[me]), (qx, qn.at[part(y)]), (ox, on.at[part(y)]),
            (tsend.at[0], trecv.at[0]), (dqx, dqr), (dkvx, dkvr))[i]
        return remote(source, target, y_send_sem.at[i], y_recv_sem.at[i], partner)

    def up_copy(b, zd):
        return remote(kv.at[b], kv.at[b], up_sem.at[b % 2, zd], kv_sem.at[b], 2 * zd + y)

    def zgrad_copy(zz):
        return remote(zsend.at[zz], zrecv.at[z], zsend_sem.at[zz], zrecv_sem.at[z], 2 * zz + y)

    def tensor_copy():
        return pltpu.make_async_remote_copy(
            tsend.at[1], trecv.at[1], t_sem.at[0], t_sem.at[1],
            device_id={"tensor": 1 - tensor}, device_id_type=MESH)

    def loop(lo, hi, body):
        def step(i, carry):
            body(i)
            return carry
        lax.fori_loop(lo, hi, step, 0)

    def column(g):
        return pl.ds(pl.multiple_of(g * D, D), D)

    barrier = pltpu.get_barrier_semaphore()
    pl.semaphore_signal(barrier, inc=1, device_id={"seq": partner}, device_id_type=MESH)
    pl.semaphore_signal(barrier, inc=1, device_id={"tensor": 1 - tensor}, device_id_type=MESH)

    def greet(step):
        other = lax.rem(z + step, half)
        pl.semaphore_signal(barrier, inc=1, device_id={"seq": 2 * other + y}, device_id_type=MESH)
    loop(1, half, greet)

    kv[me, 0] = k_ref[:, column(y)]
    kv[me, 1] = v_ref[:, column(y)]
    kvx[0] = k_ref[:, column(1 - y)]
    kvx[1] = v_ref[:, column(1 - y)]
    pl.semaphore_wait(barrier, half + 1)
    y_copy(0).start()
    loop(z + 1, half, lambda zd: up_copy(me, half + z - zd).start())

    def head_columns(g, h):
        return pl.ds(pl.multiple_of((g * GROUP + h) * D, D), D)

    for h in range(GROUP):
        qx[h * rows:(h + 1) * rows, :] = q_ref[:, head_columns(1 - y, h)]
    y_copy(1).start()
    gate = 1.0 / (1.0 + jnp.exp(-gate_ref[...]))
    gate_columns = jnp.transpose(jnp.broadcast_to(gate, (D, rows)))

    def gated(g, h):
        return (gate_columns * go_ref[:, head_columns(g, h)].astype(F32)).astype(BF16)

    for h in range(GROUP):
        ox[h * rows:(h + 1) * rows, :] = gated(1 - y, h)
    y_copy(2).start()
    for h in range(GROUP):
        queries, out_grad = q_ref[:, head_columns(y, h)], gated(y, h)
        qn[lanes(y, h), :] = queries
        on[lanes(y, h), :] = out_grad
        qt[:, lanes(y, h)] = jnp.transpose(queries)
        ot[:, lanes(y, h)] = jnp.transpose(out_grad)

    def by_slot(index, first, second):
        return jnp.where(index < BLK, first, second)

    key_row = lax.broadcasted_iota(jnp.int32, (rows, rows), 0)
    query_row = lax.broadcasted_iota(jnp.int32, (rows, rows), 1)
    query_slot = by_slot(lax.broadcasted_iota(jnp.int32, (1, rows), 1), 0, 1)
    key_slot = by_slot(key_row, 0, 1)
    live = []
    for p in range(2):
        b = 2 * z + p
        id0, id1, count = ids_ref[b, 0], ids_ref[b, 1], counts_ref[b]
        key_pos = by_slot(key_row, id0 * BLK, id1 * BLK - BLK) + key_row
        query_pos = by_slot(query_row, id0 * BLK, id1 * BLK - BLK) + query_row
        allowed = ((key_slot < count) & (key_pos <= query_pos)) | (key_row == query_row)
        bias[p] = jnp.where(allowed, 0.0, -jnp.inf).astype(F32)
        live.append(jnp.where(query_slot < count, 1.0, 0.0).astype(F32))

    def first_pass(b, p, is_own):
        keys, values = kv[b, 0], kv[b, 1]
        shut0 = jnp.where(counts_ref[b] > 0, 0.0, -jnp.inf).astype(F32)
        shut1 = jnp.where(counts_ref[b] > 1, 0.0, -jnp.inf).astype(F32)
        for h in range(GROUP):
            at = lanes(p, h)
            s = mm(keys, qt[:, at])
            if is_own:
                s = s + bias[p]
            else:
                s = jnp.concatenate([s[:BLK] + shut0, s[BLK:] + shut1], axis=0)
            prob_grads = mm(values, ot[:, at])
            top = jnp.max(s, axis=0, keepdims=True)
            if not is_own:
                before = row_max[:, at]
                top = jnp.maximum(before, top)
            e = jnp.exp2((s - top) * EXP2_SCALE)
            total = jnp.sum(e, axis=0, keepdims=True)
            dot = jnp.sum(e * prob_grads, axis=0, keepdims=True)
            if not is_own:
                shrink = jnp.exp2((before - top) * EXP2_SCALE)
                total = total + row_sum[:, at] * shrink
                dot = dot + row_dot[:, at] * shrink
            row_max[:, at] = top
            row_sum[:, at] = total
            row_dot[:, at] = dot
            block_max[b, :, at] = top
            exps[b, :, at] = e.astype(BF16)

    y_copy(0).wait_recv()
    loop(z + 1, half, lambda zd: up_copy(partner, half + z - zd).start())
    first_pass(me, y, True)
    y_copy(1).wait_recv()
    y_copy(2).wait_recv()
    for h in range(GROUP):
        qt[:, lanes(1 - y, h)] = jnp.transpose(qn[lanes(1 - y, h), :])
        ot[:, lanes(1 - y, h)] = jnp.transpose(on[lanes(1 - y, h), :])
    first_pass(partner, 1 - y, True)
    first_pass(2 * z, 1, False)

    def gather_step(i):
        b = 2 * z - 1 - i
        remote(kv.at[b], kv.at[b], up_sem.at[0, 0], kv_sem.at[b], partner).wait_recv()
        first_pass(b, 0, False)
        first_pass(b, 1, False)
    loop(0, 2 * z, gather_step)

    sums = []
    for p in range(2):
        total = jnp.zeros((1, rows), F32)
        for h in range(GROUP):
            at = lanes(p, h)
            inverse = live[p] / row_sum[:, at]
            rows_delta = row_dot[:, at] * inverse
            delta[:, at] = rows_delta
            factor[:, at] = inverse
            total = total + rows_delta
        sums.append(total)
    mine = jnp.where(y == 0, sums[0], sums[1])
    tsend[0] = jnp.broadcast_to(jnp.where(y == 0, sums[1], sums[0]), tsend.shape[1:])
    y_copy(3).start()
    dqt[...] = jnp.zeros_like(dqt)

    def score_grads(zz, kb, p):
        b = 2 * zz + kb
        values = kv[b, 1]
        row_at = slice(kb * rows, (kb + 1) * rows)
        for h in range(GROUP):
            at = slice(p * wide + h * rows, p * wide + (h + 1) * rows)
            weight = jnp.exp2((block_max[b, :, at] - row_max[:, at]) * EXP2_SCALE) * factor[:, at]
            probs = exps[b, :, at].astype(F32) * weight
            prob_grads = mm(values, ot[:, at])
            low[row_at, at] = probs.astype(BF16)
            scored[row_at, at] = (probs * (prob_grads - delta[:, at])).astype(BF16)

    def key_value_grads(kb, first):
        row_at = slice(kb * rows, (kb + 1) * rows)
        dk = mm(scored[row_at, first:], qn[first:, :]) * SCALE
        dv = mm(low[row_at, first:], on[first:, :])
        return dk, dv

    def add_query_grads(zz, key_blocks, p):
        keys_t = jnp.concatenate([jnp.transpose(kv[2 * zz + kb, 0]) for kb in key_blocks], axis=1)
        for h in range(0, GROUP, 2):
            at = slice(p * wide + h * rows, p * wide + (h + 2) * rows)
            dqt[:, at] += mm(keys_t, scored[:len(key_blocks) * rows, at])

    def pair_step(zz):
        for kb in range(2):
            for p in range(2):
                score_grads(zz, kb, p)
            dk, dv = key_value_grads(kb, 0)
            zsend[zz, kb, 0] = dk.astype(BF16)
            zsend[zz, kb, 1] = dv.astype(BF16)
        zgrad_copy(zz).start()
        for p in range(2):
            add_query_grads(zz, (0, 1), p)
    loop(0, z, pair_step)

    y_copy(3).wait_recv()
    mine = mine + trecv[0, 0:1, :]
    tsend[1] = jnp.broadcast_to(mine, tsend.shape[1:])
    tensor_copy().start()

    for kb, p in ((0, 0), (0, 1), (1, 1)):
        score_grads(z, kb, p)
    add_query_grads(z, (0,), 0)
    add_query_grads(z, (0, 1), 1)
    for h in range(GROUP):
        dqx[:, h * D:(h + 1) * D] = jnp.transpose(dqt[:, lanes(1 - y, h)] * SCALE).astype(BF16)
    y_copy(4).start()
    for kb in range(2):
        dk, dv = key_value_grads(kb, kb * wide)
        own[kb, 0] = dk
        own[kb, 1] = dv
    for h in range(GROUP):
        dq_ref[:, head_columns(y, h)] = jnp.transpose(dqt[:, lanes(y, h)] * SCALE).astype(BF16)

    def add_arrived(i):
        zs = half - 1 - i
        remote(zsend.at[zs], zrecv.at[zs], zsend_sem.at[zs], zrecv_sem.at[zs], partner).wait_recv()
        own[...] = own[...] + zrecv[zs].astype(F32)
    loop(0, half - 1 - z, add_arrived)
    dkvx[...] = own[1 - y].astype(BF16)
    y_copy(5).start()
    dk_ref[:, column(y)] = own[y, 0].astype(BF16)
    dv_ref[:, column(y)] = own[y, 1].astype(BF16)
    tensor_copy().wait_recv()
    dgate_ref[...] = (1.0 - gate) * (mine + trecv[1, 0:1, :])
    y_copy(4).wait_recv()
    dq_ref[:, pl.ds(pl.multiple_of((1 - y) * GROUP * D, GROUP * D), GROUP * D)] = dqr[...]
    y_copy(5).wait_recv()
    dk_ref[:, column(1 - y)] = dkvr[0]
    dv_ref[:, column(1 - y)] = dkvr[1]

    for i in range(6):
        y_copy(i).wait_send()
    tensor_copy().wait_send()
    loop(z + 1, half, lambda zd: up_copy(me, zd).wait_send())
    loop(z + 1, half, lambda zd: up_copy(partner, zd).wait_send())
    loop(0, z, lambda zz: zgrad_copy(zz).wait_send())


def local(n, queries, keys, values, grad_out, gate_logit, block_ids, block_counts):
    rows, width = queries.shape
    kv_width = keys.shape[1]
    assert kv_width == 2 * D and width == 2 * GROUP * D and n % 2 == 0
    half = n // 2
    wide = GROUP * rows
    vmem = pl.BlockSpec(memory_space=pltpu.VMEM)
    smem = pl.BlockSpec(memory_space=pltpu.SMEM)
    pair = (2, rows, D)
    sem = pltpu.SemaphoreType.DMA
    row = pltpu.VMEM((1, 2 * wide), F32)
    dq, dk, dv, dgate = pl.pallas_call(
        functools.partial(kernel, n),
        out_shape=(
            jax.ShapeDtypeStruct((rows, width), BF16),
            jax.ShapeDtypeStruct((rows, kv_width), BF16),
            jax.ShapeDtypeStruct((rows, kv_width), BF16),
            jax.ShapeDtypeStruct((1, rows), F32),
        ),
        in_specs=[smem, smem, vmem, vmem, vmem, vmem, vmem],
        out_specs=(vmem, vmem, vmem, vmem),
        scratch_shapes=[
            pltpu.VMEM((n,) + pair, BF16),
            pltpu.VMEM(pair, BF16),
            pltpu.VMEM((wide, D), BF16),
            pltpu.VMEM((wide, D), BF16),
            pltpu.VMEM((2 * wide, D), BF16),
            pltpu.VMEM((D, 2 * wide), BF16),
            pltpu.VMEM((2 * wide, D), BF16),
            pltpu.VMEM((D, 2 * wide), BF16),
            pltpu.VMEM((n, rows, 2 * wide), BF16),
            pltpu.VMEM((n, 1, 2 * wide), F32),
            row, row, row, row, row,
            pltpu.VMEM((D, 2 * wide), F32),
            pltpu.VMEM((2,) + pair, F32),
            pltpu.VMEM((2, rows, rows), F32),
            pltpu.VMEM((2 * rows, 2 * wide), BF16),
            pltpu.VMEM((2 * rows, 2 * wide), BF16),
            pltpu.VMEM((half, 2) + pair, BF16),
            pltpu.VMEM((half, 2) + pair, BF16),
            pltpu.VMEM((rows, GROUP * D), BF16),
            pltpu.VMEM((rows, GROUP * D), BF16),
            pltpu.VMEM(pair, BF16),
            pltpu.VMEM(pair, BF16),
            pltpu.VMEM((2, 8, rows), F32),
            pltpu.VMEM((2, 8, rows), F32),
            sem((n,)),
            sem((2, half)),
            sem((half,)),
            sem((half,)),
            sem((6,)),
            sem((6,)),
            sem((2,)),
        ],
        compiler_params=pltpu.CompilerParams(
            collective_id=0, has_side_effects=True, vmem_limit_bytes=62 * 1024 * 1024
        ),
        cost_estimate=pl.CostEstimate(
            flops=12 * n * rows * rows * width,
            bytes_accessed=6 * rows * (width + kv_width),
            transcendentals=n * rows * rows * width // D,
        ),
        name="mod_attention_grads",
    )(block_ids, block_counts, queries, keys, values, grad_out, gate_logit.reshape(1, rows))
    return dq, dk, dv, dgate.reshape(rows)


def solution(mesh):
    in_specs = (
        P(("dp", "seq"), "tensor"),
        P(("dp", "seq"), "tensor"),
        P(("dp", "seq"), "tensor"),
        P(("dp", "seq"), "tensor"),
        P(("dp", "seq")),
        P("dp", None),
        P("dp"),
    )
    out_specs = (
        P(("dp", "seq"), "tensor"),
        P(("dp", "seq"), "tensor"),
        P(("dp", "seq"), "tensor"),
        P(("dp", "seq")),
    )
    return jax.shard_map(
        functools.partial(local, mesh.shape["seq"]),
        mesh=mesh, in_specs=in_specs, out_specs=out_specs, check_vma=False,
    )
```

```python
import functools
import math

import jax
import jax.numpy as jnp
from jax import lax
from jax.experimental import pallas as pl
from jax.experimental.pallas import tpu as pltpu
from jax.sharding import PartitionSpec as P

D = 128
GROUP = 4
BLK = 128
SCALE = D ** -0.5
EXP2_SCALE = SCALE * math.log2(math.e)
MESH = pl.DeviceIdType.MESH
F32 = jnp.float32
BF16 = jnp.bfloat16


def mm(a, b):
    return jnp.dot(a, b, preferred_element_type=F32)


def kernel(
    n,
    ids_ref, counts_ref, q_ref, k_ref, v_ref, go_ref, gate_ref,
    dq_ref, dk_ref, dv_ref, dgate_ref,
    kv, kvx, qx, ox, qn, qt, on, ot, exps, block_max, row_max, row_sum, row_dot, delta, factor,
    dqt, own, bias, low, scored, zsend, zrecv, dqx, dqr, dkvx, dkvr, tsend, trecv,
    kv_sem, up_sem, zsend_sem, zrecv_sem, y_send_sem, y_recv_sem, t_sem,
):
    rows = q_ref.shape[0]
    wide = GROUP * rows
    me = lax.axis_index("seq")
    tensor = lax.axis_index("tensor")
    half = n // 2
    z, y = me // 2, me % 2
    partner = 2 * z + (1 - y)

    def remote(source, target, send_sem, recv_sem, seq):
        return pltpu.make_async_remote_copy(
            source, target, send_sem, recv_sem, device_id={"seq": seq}, device_id_type=MESH)

    def part(p):
        return pl.ds(pl.multiple_of(p * wide, wide), wide)

    def lanes(p, h):
        return pl.ds(pl.multiple_of(p * wide + h * rows, rows), rows)

    def y_copy(i):
        source, target = (
            (kvx, kv.at[me]), (qx, qn.at[part(y)]), (ox, on.at[part(y)]),
            (tsend.at[0], trecv.at[0]), (dqx, dqr), (dkvx, dkvr))[i]
        return remote(source, target, y_send_sem.at[i], y_recv_sem.at[i], partner)

    def up_copy(b):
        return remote(kv.at[b], kv.at[b], up_sem.at[b], kv_sem.at[b], me + 2)

    def pass_up(b):
        @pl.when(z < half - 1)
        def _():
            up_copy(b).start()

    def arrive(b):
        up_copy(b).wait_recv()
        pass_up(b)

    def zgrad_copy(zz):
        return remote(zsend.at[zz], zrecv.at[zz], zsend_sem.at[zz], zrecv_sem.at[zz], me - 2)

    def relay(zz):
        zgrad_copy(zz).wait_recv()
        zsend[zz] = (zsend[zz].astype(F32) + zrecv[zz].astype(F32)).astype(BF16)
        zgrad_copy(zz).start()

    def tensor_copy():
        return pltpu.make_async_remote_copy(
            tsend.at[1], trecv.at[1], t_sem.at[0], t_sem.at[1],
            device_id={"tensor": 1 - tensor}, device_id_type=MESH)

    def loop(lo, hi, body):
        def step(i, carry):
            body(i)
            return carry
        lax.fori_loop(lo, hi, step, 0)

    def column(g):
        return pl.ds(pl.multiple_of(g * D, D), D)

    barrier = pltpu.get_barrier_semaphore()
    pl.semaphore_signal(barrier, inc=1, device_id={"seq": partner}, device_id_type=MESH)
    pl.semaphore_signal(barrier, inc=1, device_id={"tensor": 1 - tensor}, device_id_type=MESH)

    @pl.when(z > 0)
    def _():
        pl.semaphore_signal(barrier, inc=1, device_id={"seq": me - 2}, device_id_type=MESH)

    @pl.when(z < half - 1)
    def _():
        pl.semaphore_signal(barrier, inc=1, device_id={"seq": me + 2}, device_id_type=MESH)

    kv[me, 0] = k_ref[:, column(y)]
    kv[me, 1] = v_ref[:, column(y)]
    kvx[0] = k_ref[:, column(1 - y)]
    kvx[1] = v_ref[:, column(1 - y)]
    has_before, has_after = (z + half - 1) // half, (2 * half - 2 - z) // half
    pl.semaphore_wait(barrier, 2 + has_before + has_after)
    y_copy(0).start()
    pass_up(me)

    def head_columns(g, h):
        return pl.ds(pl.multiple_of((g * GROUP + h) * D, D), D)

    for h in range(GROUP):
        qx[h * rows:(h + 1) * rows, :] = q_ref[:, head_columns(1 - y, h)]
    y_copy(1).start()
    gate = 1.0 / (1.0 + jnp.exp(-gate_ref[...]))
    gate_columns = jnp.transpose(jnp.broadcast_to(gate, (D, rows)))

    def gated(g, h):
        return (gate_columns * go_ref[:, head_columns(g, h)].astype(F32)).astype(BF16)

    for h in range(GROUP):
        ox[h * rows:(h + 1) * rows, :] = gated(1 - y, h)
    y_copy(2).start()
    for h in range(GROUP):
        queries, out_grad = q_ref[:, head_columns(y, h)], gated(y, h)
        qn[lanes(y, h), :] = queries
        on[lanes(y, h), :] = out_grad
        qt[:, lanes(y, h)] = jnp.transpose(queries)
        ot[:, lanes(y, h)] = jnp.transpose(out_grad)

    def by_slot(index, first, second):
        return jnp.where(index < BLK, first, second)

    key_row = lax.broadcasted_iota(jnp.int32, (rows, rows), 0)
    query_row = lax.broadcasted_iota(jnp.int32, (rows, rows), 1)
    query_slot = by_slot(lax.broadcasted_iota(jnp.int32, (1, rows), 1), 0, 1)
    key_slot = by_slot(key_row, 0, 1)
    live = []
    for p in range(2):
        b = 2 * z + p
        id0, id1, count = ids_ref[b, 0], ids_ref[b, 1], counts_ref[b]
        key_pos = by_slot(key_row, id0 * BLK, id1 * BLK - BLK) + key_row
        query_pos = by_slot(query_row, id0 * BLK, id1 * BLK - BLK) + query_row
        allowed = ((key_slot < count) & (key_pos <= query_pos)) | (key_row == query_row)
        bias[p] = jnp.where(allowed, 0.0, -jnp.inf).astype(F32)
        live.append(jnp.where(query_slot < count, 1.0, 0.0).astype(F32))

    def first_pass(b, p, is_own):
        keys, values = kv[b, 0], kv[b, 1]
        shut0 = jnp.where(counts_ref[b] > 0, 0.0, -jnp.inf).astype(F32)
        shut1 = jnp.where(counts_ref[b] > 1, 0.0, -jnp.inf).astype(F32)
        for h in range(GROUP):
            at = lanes(p, h)
            s = mm(keys, qt[:, at])
            if is_own:
                s = s + bias[p]
            else:
                s = jnp.concatenate([s[:BLK] + shut0, s[BLK:] + shut1], axis=0)
            prob_grads = mm(values, ot[:, at])
            top = jnp.max(s, axis=0, keepdims=True)
            if not is_own:
                before = row_max[:, at]
                top = jnp.maximum(before, top)
            e = jnp.exp2((s - top) * EXP2_SCALE)
            total = jnp.sum(e, axis=0, keepdims=True)
            dot = jnp.sum(e * prob_grads, axis=0, keepdims=True)
            if not is_own:
                shrink = jnp.exp2((before - top) * EXP2_SCALE)
                total = total + row_sum[:, at] * shrink
                dot = dot + row_dot[:, at] * shrink
            row_max[:, at] = top
            row_sum[:, at] = total
            row_dot[:, at] = dot
            block_max[b, :, at] = top
            exps[b, :, at] = e.astype(BF16)

    y_copy(0).wait_recv()
    pass_up(partner)
    first_pass(me, y, True)

    @pl.when(z > 0)
    def _():
        for b in (me - 2, partner - 2):
            arrive(b)
            first_pass(b, y, False)

    y_copy(1).wait_recv()
    y_copy(2).wait_recv()
    for h in range(GROUP):
        qt[:, lanes(1 - y, h)] = jnp.transpose(qn[lanes(1 - y, h), :])
        ot[:, lanes(1 - y, h)] = jnp.transpose(on[lanes(1 - y, h), :])
    first_pass(partner, 1 - y, True)
    first_pass(2 * z, 1, False)

    @pl.when(z > 0)
    def _():
        for b in (me - 2, partner - 2):
            first_pass(b, 1 - y, False)

    def gather_step(k):
        for b in (me - 2 * k, partner - 2 * k):
            arrive(b)
            first_pass(b, 0, False)
            first_pass(b, 1, False)
    loop(2, z + 1, gather_step)

    sums = []
    for p in range(2):
        total = jnp.zeros((1, rows), F32)
        for h in range(GROUP):
            at = lanes(p, h)
            inverse = live[p] / row_sum[:, at]
            rows_delta = row_dot[:, at] * inverse
            delta[:, at] = rows_delta
            factor[:, at] = inverse
            total = total + rows_delta
        sums.append(total)
    mine = jnp.where(y == 0, sums[0], sums[1])
    tsend[0] = jnp.broadcast_to(jnp.where(y == 0, sums[1], sums[0]), tsend.shape[1:])
    y_copy(3).start()
    dqt[...] = jnp.zeros_like(dqt)

    def score_grads(zz, kb, p):
        b = 2 * zz + kb
        values = kv[b, 1]
        row_at = slice(kb * rows, (kb + 1) * rows)
        for h in range(GROUP):
            at = slice(p * wide + h * rows, p * wide + (h + 1) * rows)
            weight = jnp.exp2((block_max[b, :, at] - row_max[:, at]) * EXP2_SCALE) * factor[:, at]
            probs = exps[b, :, at].astype(F32) * weight
            prob_grads = mm(values, ot[:, at])
            low[row_at, at] = probs.astype(BF16)
            scored[row_at, at] = (probs * (prob_grads - delta[:, at])).astype(BF16)

    def key_value_grads(kb, first):
        row_at = slice(kb * rows, (kb + 1) * rows)
        dk = mm(scored[row_at, first:], qn[first:, :]) * SCALE
        dv = mm(low[row_at, first:], on[first:, :])
        return dk, dv

    def add_query_grads(zz, key_blocks, p):
        keys_t = jnp.concatenate([jnp.transpose(kv[2 * zz + kb, 0]) for kb in key_blocks], axis=1)
        for h in range(0, GROUP, 2):
            at = slice(p * wide + h * rows, p * wide + (h + 2) * rows)
            dqt[:, at] += mm(keys_t, scored[:len(key_blocks) * rows, at])

    def pair_step(zz):
        for kb in range(2):
            for p in range(2):
                score_grads(zz, kb, p)
            dk, dv = key_value_grads(kb, 0)
            zsend[zz, kb, 0] = dk.astype(BF16)
            zsend[zz, kb, 1] = dv.astype(BF16)

        @pl.when(z == half - 1)
        def _():
            zgrad_copy(zz).start()

        for p in range(2):
            add_query_grads(zz, (0, 1), p)
    loop(0, z, pair_step)
    next_to_last = (z == half - 2) & (z > 0)

    @pl.when(next_to_last)
    def _():
        relay(0)

    y_copy(3).wait_recv()
    mine = mine + trecv[0, 0:1, :]
    tsend[1] = jnp.broadcast_to(mine, tsend.shape[1:])
    tensor_copy().start()

    for kb, p in ((0, 0), (0, 1), (1, 1)):
        score_grads(z, kb, p)
    add_query_grads(z, (0,), 0)
    add_query_grads(z, (0, 1), 1)
    for h in range(GROUP):
        dqx[:, h * D:(h + 1) * D] = jnp.transpose(dqt[:, lanes(1 - y, h)] * SCALE).astype(BF16)
    y_copy(4).start()
    for kb in range(2):
        dk, dv = key_value_grads(kb, kb * wide)
        own[kb, 0] = dk
        own[kb, 1] = dv
    for h in range(GROUP):
        dq_ref[:, head_columns(y, h)] = jnp.transpose(dqt[:, lanes(y, h)] * SCALE).astype(BF16)

    @pl.when(z < half - 1)
    def _():
        loop(jnp.where(next_to_last, 1, 0), z, relay)
        zgrad_copy(z).wait_recv()
        own[...] = own[...] + zrecv[z].astype(F32)

    dkvx[...] = own[1 - y].astype(BF16)
    y_copy(5).start()
    dk_ref[:, column(y)] = own[y, 0].astype(BF16)
    dv_ref[:, column(y)] = own[y, 1].astype(BF16)
    tensor_copy().wait_recv()
    dgate_ref[...] = (1.0 - gate) * (mine + trecv[1, 0:1, :])
    y_copy(4).wait_recv()
    dq_ref[:, pl.ds(pl.multiple_of((1 - y) * GROUP * D, GROUP * D), GROUP * D)] = dqr[...]
    y_copy(5).wait_recv()
    dk_ref[:, column(1 - y)] = dkvr[0]
    dv_ref[:, column(1 - y)] = dkvr[1]

    for i in range(6):
        y_copy(i).wait_send()
    tensor_copy().wait_send()

    @pl.when(z < half - 1)
    def _():
        loop(0, 2 * z + 2, lambda b: up_copy(b).wait_send())

    loop(0, z, lambda zz: zgrad_copy(zz).wait_send())


def local(n, queries, keys, values, grad_out, gate_logit, block_ids, block_counts):
    rows, width = queries.shape
    kv_width = keys.shape[1]
    assert kv_width == 2 * D and width == 2 * GROUP * D and n % 2 == 0
    half = n // 2
    wide = GROUP * rows
    vmem = pl.BlockSpec(memory_space=pltpu.VMEM)
    smem = pl.BlockSpec(memory_space=pltpu.SMEM)
    pair = (2, rows, D)
    sem = pltpu.SemaphoreType.DMA
    row = pltpu.VMEM((1, 2 * wide), F32)
    dq, dk, dv, dgate = pl.pallas_call(
        functools.partial(kernel, n),
        out_shape=(
            jax.ShapeDtypeStruct((rows, width), BF16),
            jax.ShapeDtypeStruct((rows, kv_width), BF16),
            jax.ShapeDtypeStruct((rows, kv_width), BF16),
            jax.ShapeDtypeStruct((1, rows), F32),
        ),
        in_specs=[smem, smem, vmem, vmem, vmem, vmem, vmem],
        out_specs=(vmem, vmem, vmem, vmem),
        scratch_shapes=[
            pltpu.VMEM((n,) + pair, BF16),
            pltpu.VMEM(pair, BF16),
            pltpu.VMEM((wide, D), BF16),
            pltpu.VMEM((wide, D), BF16),
            pltpu.VMEM((2 * wide, D), BF16),
            pltpu.VMEM((D, 2 * wide), BF16),
            pltpu.VMEM((2 * wide, D), BF16),
            pltpu.VMEM((D, 2 * wide), BF16),
            pltpu.VMEM((n, rows, 2 * wide), BF16),
            pltpu.VMEM((n, 1, 2 * wide), F32),
            row, row, row, row, row,
            pltpu.VMEM((D, 2 * wide), F32),
            pltpu.VMEM((2,) + pair, F32),
            pltpu.VMEM((2, rows, rows), F32),
            pltpu.VMEM((2 * rows, 2 * wide), BF16),
            pltpu.VMEM((2 * rows, 2 * wide), BF16),
            pltpu.VMEM((half, 2) + pair, BF16),
            pltpu.VMEM((half, 2) + pair, BF16),
            pltpu.VMEM((rows, GROUP * D), BF16),
            pltpu.VMEM((rows, GROUP * D), BF16),
            pltpu.VMEM(pair, BF16),
            pltpu.VMEM(pair, BF16),
            pltpu.VMEM((2, 8, rows), F32),
            pltpu.VMEM((2, 8, rows), F32),
            sem((n,)),
            sem((n,)),
            sem((half,)),
            sem((half,)),
            sem((6,)),
            sem((6,)),
            sem((2,)),
        ],
        compiler_params=pltpu.CompilerParams(
            collective_id=0, has_side_effects=True, vmem_limit_bytes=62 * 1024 * 1024
        ),
        cost_estimate=pl.CostEstimate(
            flops=12 * n * rows * rows * width,
            bytes_accessed=6 * rows * (width + kv_width),
            transcendentals=n * rows * rows * width // D,
        ),
        name="mod_attention_grads",
    )(block_ids, block_counts, queries, keys, values, grad_out, gate_logit.reshape(1, rows))
    return dq, dk, dv, dgate.reshape(rows)


def solution(mesh):
    in_specs = (
        P(("dp", "seq"), "tensor"),
        P(("dp", "seq"), "tensor"),
        P(("dp", "seq"), "tensor"),
        P(("dp", "seq"), "tensor"),
        P(("dp", "seq")),
        P("dp", None),
        P("dp"),
    )
    out_specs = (
        P(("dp", "seq"), "tensor"),
        P(("dp", "seq"), "tensor"),
        P(("dp", "seq"), "tensor"),
        P(("dp", "seq")),
    )
    return jax.shard_map(
        functools.partial(local, mesh.shape["seq"]),
        mesh=mesh, in_specs=in_specs, out_specs=out_specs, check_vma=False,
    )
```

```python
import functools
import math

import jax
import jax.numpy as jnp
from jax import lax
from jax.experimental import pallas as pl
from jax.experimental.pallas import tpu as pltpu
from jax.sharding import PartitionSpec as P

D = 128
GROUP = 4
BLK = 128
SCALE = D ** -0.5
EXP2_SCALE = SCALE * math.log2(math.e)
MESH = pl.DeviceIdType.MESH
F32 = jnp.float32
BF16 = jnp.bfloat16


def mm(a, b):
    return jnp.dot(a, b, preferred_element_type=F32)


def kernel(
    n,
    ids_ref, counts_ref, q_ref, k_ref, v_ref, go_ref, gate_ref,
    dq_ref, dk_ref, dv_ref, dgate_ref,
    kv, kvx, qx, ox, qn, qt, on, ot, exps, block_max, row_max, row_sum, row_out, delta, factor,
    dqt, own, bias, low, scored, zsend, zrecv, dqx, dqr, dkvx, dkvr, tsend, trecv,
    kv_sem, up_sem, zsend_sem, zrecv_sem, y_send_sem, y_recv_sem, t_sem,
):
    rows = q_ref.shape[0]
    wide = GROUP * rows
    me = lax.axis_index("seq")
    tensor = lax.axis_index("tensor")
    half = n // 2
    z, y = me // 2, me % 2
    partner = 2 * z + (1 - y)

    def remote(source, target, send_sem, recv_sem, seq):
        return pltpu.make_async_remote_copy(
            source, target, send_sem, recv_sem, device_id={"seq": seq}, device_id_type=MESH)

    def part(p):
        return pl.ds(pl.multiple_of(p * wide, wide), wide)

    def lanes(p, h):
        return pl.ds(pl.multiple_of(p * wide + h * rows, rows), rows)

    def y_copy(i):
        source, target = (
            (kvx, kv.at[me]), (qx, qn.at[part(y)]), (ox, on.at[part(y)]),
            (tsend.at[0], trecv.at[0]), (dqx, dqr), (dkvx, dkvr))[i]
        return remote(source, target, y_send_sem.at[i], y_recv_sem.at[i], partner)

    def up_copy(b):
        return remote(kv.at[b], kv.at[b], up_sem.at[b], kv_sem.at[b], me + 2)

    def pass_up(b):
        @pl.when(z < half - 1)
        def _():
            up_copy(b).start()

    def arrive(b):
        up_copy(b).wait_recv()
        pass_up(b)

    def zgrad_copy(zz):
        return remote(zsend.at[zz], zrecv.at[zz], zsend_sem.at[zz], zrecv_sem.at[zz], me - 2)

    def relay(zz):
        zgrad_copy(zz).wait_recv()
        zsend[zz] = (zsend[zz].astype(F32) + zrecv[zz].astype(F32)).astype(BF16)
        zgrad_copy(zz).start()

    def tensor_copy():
        return pltpu.make_async_remote_copy(
            tsend.at[1], trecv.at[1], t_sem.at[0], t_sem.at[1],
            device_id={"tensor": 1 - tensor}, device_id_type=MESH)

    def loop(lo, hi, body):
        def step(i, carry):
            body(i)
            return carry
        lax.fori_loop(lo, hi, step, 0)

    def column(g):
        return pl.ds(pl.multiple_of(g * D, D), D)

    barrier = pltpu.get_barrier_semaphore()
    pl.semaphore_signal(barrier, inc=1, device_id={"seq": partner}, device_id_type=MESH)
    pl.semaphore_signal(barrier, inc=1, device_id={"tensor": 1 - tensor}, device_id_type=MESH)

    @pl.when(z > 0)
    def _():
        pl.semaphore_signal(barrier, inc=1, device_id={"seq": me - 2}, device_id_type=MESH)

    @pl.when(z < half - 1)
    def _():
        pl.semaphore_signal(barrier, inc=1, device_id={"seq": me + 2}, device_id_type=MESH)

    kv[me, 0] = k_ref[:, column(y)]
    kv[me, 1] = v_ref[:, column(y)]
    kvx[0] = k_ref[:, column(1 - y)]
    kvx[1] = v_ref[:, column(1 - y)]
    has_before, has_after = (z + half - 1) // half, (2 * half - 2 - z) // half
    pl.semaphore_wait(barrier, 2 + has_before + has_after)
    y_copy(0).start()
    pass_up(me)

    def head_columns(g, h):
        return pl.ds(pl.multiple_of((g * GROUP + h) * D, D), D)

    for h in range(GROUP):
        qx[h * rows:(h + 1) * rows, :] = q_ref[:, head_columns(1 - y, h)]
    y_copy(1).start()
    gate = 1.0 / (1.0 + jnp.exp(-gate_ref[...]))
    gate_columns = jnp.transpose(jnp.broadcast_to(gate, (D, rows)))

    def gated(g, h):
        return (gate_columns * go_ref[:, head_columns(g, h)].astype(F32)).astype(BF16)

    for h in range(GROUP):
        ox[h * rows:(h + 1) * rows, :] = gated(1 - y, h)
    y_copy(2).start()
    for h in range(GROUP):
        queries, out_grad = q_ref[:, head_columns(y, h)], gated(y, h)
        qn[lanes(y, h), :] = queries
        on[lanes(y, h), :] = out_grad
        qt[:, lanes(y, h)] = jnp.transpose(queries)
        ot[:, lanes(y, h)] = jnp.transpose(out_grad)

    def by_slot(index, first, second):
        return jnp.where(index < BLK, first, second)

    key_row = lax.broadcasted_iota(jnp.int32, (rows, rows), 0)
    query_row = lax.broadcasted_iota(jnp.int32, (rows, rows), 1)
    query_slot = by_slot(lax.broadcasted_iota(jnp.int32, (1, rows), 1), 0, 1)
    key_slot = by_slot(key_row, 0, 1)
    live = []
    for p in range(2):
        b = 2 * z + p
        id0, id1, count = ids_ref[0, b], ids_ref[1, b], counts_ref[b]
        key_pos = by_slot(key_row, id0 * BLK, id1 * BLK - BLK) + key_row
        query_pos = by_slot(query_row, id0 * BLK, id1 * BLK - BLK) + query_row
        allowed = ((key_slot < count) & (key_pos <= query_pos)) | (key_row == query_row)
        bias[p] = jnp.where(allowed, 0.0, -jnp.inf).astype(F32)
        live.append(jnp.where(query_slot < count, 1.0, 0.0).astype(F32))

    def first_pass(b, p, is_own):
        keys, values_t = kv[b, 0], jnp.transpose(kv[b, 1])
        shut0 = jnp.where(counts_ref[b] > 0, 0.0, -jnp.inf).astype(F32)
        shut1 = jnp.where(counts_ref[b] > 1, 0.0, -jnp.inf).astype(F32)
        for h in range(GROUP):
            at = slice(p * wide + h * rows, p * wide + (h + 1) * rows)
            s = mm(keys, qt[:, at])
            if is_own:
                s = s + bias[p]
            else:
                s = jnp.concatenate([s[:BLK] + shut0, s[BLK:] + shut1], axis=0)
            top = jnp.max(s, axis=0, keepdims=True)
            if not is_own:
                before = row_max[:, at]
                top = jnp.maximum(before, top)
            e = jnp.exp2((s - top) * EXP2_SCALE)
            total = jnp.sum(e, axis=0, keepdims=True)
            low_e = e.astype(BF16)
            weighted = mm(values_t, low_e)
            if not is_own:
                shrink = jnp.exp2((before - top) * EXP2_SCALE)
                total = total + row_sum[:, at] * shrink
                weighted = weighted + row_out[:, at] * shrink
            row_max[:, at] = top
            row_sum[:, at] = total
            row_out[:, at] = weighted
            block_max[b, :, at] = top
            exps[b, :, at] = low_e

    def for_shard(parity, body):
        for p in range(2):
            pl.when(parity == p)(functools.partial(body, p))

    y_copy(0).wait_recv()
    pass_up(partner)
    for_shard(y, lambda p: first_pass(me, p, True))

    def early(p):
        for b in (me - 2, partner - 2):
            arrive(b)
            first_pass(b, p, False)

    def late(p):
        first_pass(partner, p, True)

    def late_before(p):
        for b in (me - 2, partner - 2):
            first_pass(b, p, False)

    @pl.when(z > 0)
    def _():
        for_shard(y, early)
    y_copy(1).wait_recv()
    for h in range(GROUP):
        qt[:, lanes(1 - y, h)] = jnp.transpose(qn[lanes(1 - y, h), :])
    for_shard(1 - y, late)
    first_pass(2 * z, 1, False)

    @pl.when(z > 0)
    def _():
        for_shard(1 - y, late_before)

    def gather_step(k):
        for b in (me - 2 * k, partner - 2 * k):
            arrive(b)
            first_pass(b, 0, False)
            first_pass(b, 1, False)
    loop(2, z + 1, gather_step)

    y_copy(2).wait_recv()
    for h in range(GROUP):
        ot[:, lanes(1 - y, h)] = jnp.transpose(on[lanes(1 - y, h), :])
    sums = []
    for p in range(2):
        total = jnp.zeros((1, rows), F32)
        for h in range(GROUP):
            at = lanes(p, h)
            inverse = live[p] / row_sum[:, at]
            dot = jnp.sum(row_out[:, at] * ot[:, at].astype(F32), axis=0, keepdims=True)
            rows_delta = dot * inverse
            delta[:, at] = rows_delta
            factor[:, at] = inverse
            total = total + rows_delta
        sums.append(total)
    mine = jnp.where(y == 0, sums[0], sums[1])
    tsend[0] = jnp.broadcast_to(jnp.where(y == 0, sums[1], sums[0]), tsend.shape[1:])
    y_copy(3).start()
    dqt[...] = jnp.zeros_like(dqt)

    def score_grads(zz, kb, p):
        b = 2 * zz + kb
        values = kv[b, 1]
        row_at = slice(kb * rows, (kb + 1) * rows)
        for h in range(GROUP):
            at = slice(p * wide + h * rows, p * wide + (h + 1) * rows)
            weight = jnp.exp2((block_max[b, :, at] - row_max[:, at]) * EXP2_SCALE) * factor[:, at]
            probs = exps[b, :, at].astype(F32) * weight
            prob_grads = mm(values, ot[:, at])
            low[row_at, at] = probs.astype(BF16)
            scored[row_at, at] = (probs * (prob_grads - delta[:, at])).astype(BF16)

    def key_value_grads(kb, first):
        row_at = slice(kb * rows, (kb + 1) * rows)
        dk = mm(scored[row_at, first:], qn[first:, :]) * SCALE
        dv = mm(low[row_at, first:], on[first:, :])
        return dk, dv

    def add_query_grads(zz, key_blocks, p):
        keys_t = jnp.concatenate([jnp.transpose(kv[2 * zz + kb, 0]) for kb in key_blocks], axis=1)
        for h in range(0, GROUP, 2):
            at = slice(p * wide + h * rows, p * wide + (h + 2) * rows)
            dqt[:, at] += mm(keys_t, scored[:len(key_blocks) * rows, at])

    def pair_step(zz):
        for kb in range(2):
            for p in range(2):
                score_grads(zz, kb, p)
            dk, dv = key_value_grads(kb, 0)
            zsend[zz, kb, 0] = dk.astype(BF16)
            zsend[zz, kb, 1] = dv.astype(BF16)

        @pl.when(z == half - 1)
        def _():
            zgrad_copy(zz).start()

        for p in range(2):
            add_query_grads(zz, (0, 1), p)
    loop(0, z, pair_step)
    next_to_last = (z == half - 2) & (z > 0)

    @pl.when(next_to_last)
    def _():
        relay(0)

    y_copy(3).wait_recv()
    mine = mine + trecv[0, 0:1, :]
    tsend[1] = jnp.broadcast_to(mine, tsend.shape[1:])
    tensor_copy().start()

    for kb, p in ((0, 0), (0, 1), (1, 1)):
        score_grads(z, kb, p)
    add_query_grads(z, (0,), 0)
    add_query_grads(z, (0, 1), 1)
    for h in range(GROUP):
        dqx[:, h * D:(h + 1) * D] = jnp.transpose(dqt[:, lanes(1 - y, h)] * SCALE).astype(BF16)
    y_copy(4).start()
    for kb in range(2):
        dk, dv = key_value_grads(kb, kb * wide)
        own[kb, 0] = dk
        own[kb, 1] = dv
    for h in range(GROUP):
        dq_ref[:, head_columns(y, h)] = jnp.transpose(dqt[:, lanes(y, h)] * SCALE).astype(BF16)

    @pl.when(z < half - 1)
    def _():
        loop(jnp.where(next_to_last, 1, 0), z, relay)
        zgrad_copy(z).wait_recv()
        own[...] = own[...] + zrecv[z].astype(F32)

    dkvx[...] = own[1 - y].astype(BF16)
    y_copy(5).start()
    dk_ref[:, column(y)] = own[y, 0].astype(BF16)
    dv_ref[:, column(y)] = own[y, 1].astype(BF16)
    tensor_copy().wait_recv()
    dgate_ref[...] = (1.0 - gate) * (mine + trecv[1, 0:1, :])
    y_copy(4).wait_recv()
    dq_ref[:, pl.ds(pl.multiple_of((1 - y) * GROUP * D, GROUP * D), GROUP * D)] = dqr[...]
    y_copy(5).wait_recv()
    dk_ref[:, column(1 - y)] = dkvr[0]
    dv_ref[:, column(1 - y)] = dkvr[1]

    for i in range(6):
        y_copy(i).wait_send()
    tensor_copy().wait_send()

    @pl.when(z < half - 1)
    def _():
        loop(0, 2 * z + 2, lambda b: up_copy(b).wait_send())

    loop(0, z, lambda zz: zgrad_copy(zz).wait_send())


def hand_over(*refs):
    count = (len(refs) - 1) // 2
    sems = refs[-1]
    copies = []
    for source, target in zip(refs[:count], refs[count:-1]):
        rows = source.shape[0]
        step = rows // 4 if rows * source.shape[1] > 2 ** 17 else rows
        for first in range(0, rows, step):
            at = pl.ds(first, step)
            copies.append(pltpu.make_async_copy(source.at[at], target.at[at], sems.at[len(copies)]))
    for copy in copies:
        copy.start()
    for copy in copies:
        copy.wait()


def local(n, queries, keys, values, grad_out, gate_logit, block_ids, block_counts):
    rows, width = queries.shape
    kv_width = keys.shape[1]
    assert kv_width == 2 * D and width == 2 * GROUP * D and n % 2 == 0
    half = n // 2
    wide = GROUP * rows
    vmem = pl.BlockSpec(memory_space=pltpu.VMEM)
    smem = pl.BlockSpec(memory_space=pltpu.SMEM)
    pair = (2, rows, D)
    sem = pltpu.SemaphoreType.DMA
    row = pltpu.VMEM((1, 2 * wide), F32)
    dq, dk, dv, dgate = pl.pallas_call(
        functools.partial(kernel, n),
        out_shape=(
            jax.ShapeDtypeStruct((rows, width), BF16),
            jax.ShapeDtypeStruct((rows, kv_width), BF16),
            jax.ShapeDtypeStruct((rows, kv_width), BF16),
            jax.ShapeDtypeStruct((1, rows), F32),
        ),
        in_specs=[smem, smem, vmem, vmem, vmem, vmem, vmem],
        out_specs=(vmem, vmem, vmem, vmem),
        scratch_shapes=[
            pltpu.VMEM((n,) + pair, BF16),
            pltpu.VMEM(pair, BF16),
            pltpu.VMEM((wide, D), BF16),
            pltpu.VMEM((wide, D), BF16),
            pltpu.VMEM((2 * wide, D), BF16),
            pltpu.VMEM((D, 2 * wide), BF16),
            pltpu.VMEM((2 * wide, D), BF16),
            pltpu.VMEM((D, 2 * wide), BF16),
            pltpu.VMEM((n, rows, 2 * wide), BF16),
            pltpu.VMEM((n, 1, 2 * wide), F32),
            row, row,
            pltpu.VMEM((D, 2 * wide), F32),
            row, row,
            pltpu.VMEM((D, 2 * wide), F32),
            pltpu.VMEM((2,) + pair, F32),
            pltpu.VMEM((2, rows, rows), F32),
            pltpu.VMEM((2 * rows, 2 * wide), BF16),
            pltpu.VMEM((2 * rows, 2 * wide), BF16),
            pltpu.VMEM((half, 2) + pair, BF16),
            pltpu.VMEM((half, 2) + pair, BF16),
            pltpu.VMEM((rows, GROUP * D), BF16),
            pltpu.VMEM((rows, GROUP * D), BF16),
            pltpu.VMEM(pair, BF16),
            pltpu.VMEM(pair, BF16),
            pltpu.VMEM((2, 8, rows), F32),
            pltpu.VMEM((2, 8, rows), F32),
            sem((n,)),
            sem((n,)),
            sem((half,)),
            sem((half,)),
            sem((6,)),
            sem((6,)),
            sem((2,)),
        ],
        compiler_params=pltpu.CompilerParams(
            collective_id=0, has_side_effects=True, vmem_limit_bytes=62 * 1024 * 1024
        ),
        cost_estimate=pl.CostEstimate(
            flops=12 * n * rows * rows * width,
            bytes_accessed=6 * rows * (width + kv_width),
            transcendentals=n * rows * rows * width // D,
        ),
        name="mod_attention_grads",
    )(block_ids.T, block_counts, queries, keys, values, grad_out, gate_logit.reshape(1, rows))
    results = (dq, dk, dv, dgate)
    anywhere = pl.BlockSpec(memory_space=pl.ANY)
    dq, dk, dv, dgate = pl.pallas_call(
        hand_over,
        out_shape=tuple(jax.ShapeDtypeStruct(x.shape, x.dtype) for x in results),
        in_specs=[anywhere] * 4,
        out_specs=(anywhere,) * 4,
        scratch_shapes=[sem((7,))],
        name="hand_over",
    )(*results)
    return dq, dk, dv, dgate.reshape(rows)


def solution(mesh):
    in_specs = (
        P(("dp", "seq"), "tensor"),
        P(("dp", "seq"), "tensor"),
        P(("dp", "seq"), "tensor"),
        P(("dp", "seq"), "tensor"),
        P(("dp", "seq")),
        P("dp", None),
        P("dp"),
    )
    out_specs = (
        P(("dp", "seq"), "tensor"),
        P(("dp", "seq"), "tensor"),
        P(("dp", "seq"), "tensor"),
        P(("dp", "seq")),
    )
    return jax.shard_map(
        functools.partial(local, mesh.shape["seq"]),
        mesh=mesh, in_specs=in_specs, out_specs=out_specs, check_vma=False,
    )
```

```python
import functools
import math

import jax
import jax.numpy as jnp
from jax import lax
from jax.experimental import pallas as pl
from jax.experimental.pallas import tpu as pltpu
from jax.sharding import PartitionSpec as P

D = 128
GROUP = 4
BLK = 128
SCALE = D ** -0.5
EXP2_SCALE = SCALE * math.log2(math.e)
MESH = pl.DeviceIdType.MESH
F32 = jnp.float32
BF16 = jnp.bfloat16


def mm(a, b):
    return jnp.dot(a, b, preferred_element_type=F32)


def kernel(
    n,
    ids_ref, counts_ref, q_ref, k_ref, v_ref, go_ref, gate_ref,
    dq_ref, dk_ref, dv_ref, dgate_ref,
    kv, kvx, qx, ox, qn, qt, on, ot, exps, block_max, row_max, row_sum, row_out, delta, factor,
    dqt, own, bias, low, scored, zsend, zrecv, dqx, dqr, dkvx, dkvr, tsend, trecv,
    kv_sem, up_sem, zsend_sem, zrecv_sem, y_send_sem, y_recv_sem, t_sem,
):
    rows = q_ref.shape[0]
    wide = GROUP * rows
    me = lax.axis_index("seq")
    tensor = lax.axis_index("tensor")
    half = n // 2
    z, y = me // 2, me % 2
    partner = 2 * z + (1 - y)

    def remote(source, target, send_sem, recv_sem, seq):
        return pltpu.make_async_remote_copy(
            source, target, send_sem, recv_sem, device_id={"seq": seq}, device_id_type=MESH)

    def part(p):
        return pl.ds(pl.multiple_of(p * wide, wide), wide)

    def lanes(p, h):
        return pl.ds(pl.multiple_of(p * wide + h * rows, rows), rows)

    def y_copy(i):
        source, target = (
            (kvx, kv.at[me]), (qx, qn.at[part(y)]), (ox, on.at[part(y)]),
            (tsend.at[0], trecv.at[0]), (dqx, dqr), (dkvx, dkvr))[i]
        return remote(source, target, y_send_sem.at[i], y_recv_sem.at[i], partner)

    def up_copy(b):
        return remote(kv.at[b], kv.at[b], up_sem.at[b], kv_sem.at[b], me + 2)

    def pass_up(b):
        @pl.when(z < half - 1)
        def _():
            up_copy(b).start()

    def arrive(b):
        up_copy(b).wait_recv()
        pass_up(b)

    def zgrad_copy(b):
        return remote(zsend.at[b], zrecv.at[b], zsend_sem.at[b], zrecv_sem.at[b], me - 2)

    def relay(b):
        zgrad_copy(b).wait_recv()
        zsend[b] = (zsend[b].astype(F32) + zrecv[b].astype(F32)).astype(BF16)
        zgrad_copy(b).start()

    def tensor_copy():
        return pltpu.make_async_remote_copy(
            tsend.at[1], trecv.at[1], t_sem.at[0], t_sem.at[1],
            device_id={"tensor": 1 - tensor}, device_id_type=MESH)

    def loop(lo, hi, body):
        def step(i, carry):
            body(i)
            return carry
        lax.fori_loop(lo, hi, step, 0)

    def column(g):
        return pl.ds(pl.multiple_of(g * D, D), D)

    barrier = pltpu.get_barrier_semaphore()
    pl.semaphore_signal(barrier, inc=1, device_id={"seq": partner}, device_id_type=MESH)
    pl.semaphore_signal(barrier, inc=1, device_id={"tensor": 1 - tensor}, device_id_type=MESH)

    @pl.when(z > 0)
    def _():
        pl.semaphore_signal(barrier, inc=1, device_id={"seq": me - 2}, device_id_type=MESH)

    @pl.when(z < half - 1)
    def _():
        pl.semaphore_signal(barrier, inc=1, device_id={"seq": me + 2}, device_id_type=MESH)

    kv[me, 0] = k_ref[:, column(y)]
    kv[me, 1] = v_ref[:, column(y)]
    kvx[0] = k_ref[:, column(1 - y)]
    kvx[1] = v_ref[:, column(1 - y)]
    has_before, has_after = (z + half - 1) // half, (2 * half - 2 - z) // half
    pl.semaphore_wait(barrier, 2 + has_before + has_after)
    y_copy(0).start()
    pass_up(me)

    def head_columns(g, h):
        return pl.ds(pl.multiple_of((g * GROUP + h) * D, D), D)

    for h in range(GROUP):
        qx[h * rows:(h + 1) * rows, :] = q_ref[:, head_columns(1 - y, h)]
    y_copy(1).start()
    gate = 1.0 / (1.0 + jnp.exp(-gate_ref[...]))
    gate_columns = jnp.transpose(jnp.broadcast_to(gate, (D, rows)))

    def gated(g, h):
        return (gate_columns * go_ref[:, head_columns(g, h)].astype(F32)).astype(BF16)

    for h in range(GROUP):
        ox[h * rows:(h + 1) * rows, :] = gated(1 - y, h)
    y_copy(2).start()
    for h in range(GROUP):
        queries, out_grad = q_ref[:, head_columns(y, h)], gated(y, h)
        qn[lanes(y, h), :] = queries
        on[lanes(y, h), :] = out_grad
        qt[:, lanes(y, h)] = jnp.transpose(queries)
        ot[:, lanes(y, h)] = jnp.transpose(out_grad)

    def by_slot(index, first, second):
        return jnp.where(index < BLK, first, second)

    key_row = lax.broadcasted_iota(jnp.int32, (rows, rows), 0)
    query_row = lax.broadcasted_iota(jnp.int32, (rows, rows), 1)
    query_slot = by_slot(lax.broadcasted_iota(jnp.int32, (1, rows), 1), 0, 1)
    key_slot = by_slot(key_row, 0, 1)
    live = []
    for p in range(2):
        b = 2 * z + p
        id0, id1, count = ids_ref[0, b], ids_ref[1, b], counts_ref[b]
        key_pos = by_slot(key_row, id0 * BLK, id1 * BLK - BLK) + key_row
        query_pos = by_slot(query_row, id0 * BLK, id1 * BLK - BLK) + query_row
        allowed = ((key_slot < count) & (key_pos <= query_pos)) | (key_row == query_row)
        bias[p] = jnp.where(allowed, 0.0, -jnp.inf).astype(F32)
        live.append(jnp.where(query_slot < count, 1.0, 0.0).astype(F32))

    def first_pass(b, p, is_own):
        keys, values_t = kv[b, 0], jnp.transpose(kv[b, 1])
        shut0 = jnp.where(counts_ref[b] > 0, 0.0, -jnp.inf).astype(F32)
        shut1 = jnp.where(counts_ref[b] > 1, 0.0, -jnp.inf).astype(F32)
        for h in range(GROUP):
            at = slice(p * wide + h * rows, p * wide + (h + 1) * rows)
            s = mm(keys, qt[:, at])
            if is_own:
                s = s + bias[p]
            else:
                s = jnp.concatenate([s[:BLK] + shut0, s[BLK:] + shut1], axis=0)
            top = jnp.max(s, axis=0, keepdims=True)
            if not is_own:
                before = row_max[:, at]
                top = jnp.maximum(before, top)
            e = jnp.exp2((s - top) * EXP2_SCALE)
            total = jnp.sum(e, axis=0, keepdims=True)
            low_e = e.astype(BF16)
            weighted = mm(values_t, low_e)
            if not is_own:
                shrink = jnp.exp2((before - top) * EXP2_SCALE)
                total = total + row_sum[:, at] * shrink
                weighted = weighted + row_out[:, at] * shrink
            row_max[:, at] = top
            row_sum[:, at] = total
            row_out[:, at] = weighted
            block_max[b, :, at] = top
            exps[b, :, at] = low_e

    def for_shard(parity, body):
        for p in range(2):
            pl.when(parity == p)(functools.partial(body, p))

    y_copy(0).wait_recv()
    pass_up(partner)
    for_shard(y, lambda p: first_pass(me, p, True))

    def early(p):
        for b in (me - 2, partner - 2):
            arrive(b)
            first_pass(b, p, False)

    def late(p):
        first_pass(partner, p, True)

    def late_before(p):
        for b in (me - 2, partner - 2):
            first_pass(b, p, False)

    @pl.when(z > 0)
    def _():
        for_shard(y, early)
    y_copy(1).wait_recv()
    for h in range(GROUP):
        qt[:, lanes(1 - y, h)] = jnp.transpose(qn[lanes(1 - y, h), :])
    for_shard(1 - y, late)
    first_pass(2 * z, 1, False)

    @pl.when(z > 0)
    def _():
        for_shard(1 - y, late_before)

    def gather_step(k):
        for b in (me - 2 * k, partner - 2 * k):
            arrive(b)
            first_pass(b, 0, False)
            first_pass(b, 1, False)
    loop(2, z + 1, gather_step)

    y_copy(2).wait_recv()
    for h in range(GROUP):
        ot[:, lanes(1 - y, h)] = jnp.transpose(on[lanes(1 - y, h), :])
    sums = []
    for p in range(2):
        total = jnp.zeros((1, rows), F32)
        for h in range(GROUP):
            at = lanes(p, h)
            inverse = live[p] / row_sum[:, at]
            dot = jnp.sum(row_out[:, at] * ot[:, at].astype(F32), axis=0, keepdims=True)
            rows_delta = dot * inverse
            delta[:, at] = rows_delta
            factor[:, at] = inverse
            total = total + rows_delta
        sums.append(total)
    mine = jnp.where(y == 0, sums[0], sums[1])
    tsend[0] = jnp.broadcast_to(jnp.where(y == 0, sums[1], sums[0]), tsend.shape[1:])
    y_copy(3).start()
    dqt[...] = jnp.zeros_like(dqt)

    def score_grads(zz, kb, p):
        b = 2 * zz + kb
        values = kv[b, 1]
        row_at = slice(kb * rows, (kb + 1) * rows)
        for h in range(GROUP):
            at = slice(p * wide + h * rows, p * wide + (h + 1) * rows)
            weight = jnp.exp2((block_max[b, :, at] - row_max[:, at]) * EXP2_SCALE) * factor[:, at]
            probs = exps[b, :, at].astype(F32) * weight
            prob_grads = mm(values, ot[:, at])
            low[row_at, at] = probs.astype(BF16)
            scored[row_at, at] = (probs * (prob_grads - delta[:, at])).astype(BF16)

    def key_value_grads(kb, first):
        row_at = slice(kb * rows, (kb + 1) * rows)
        dk = mm(scored[row_at, first:], qn[first:, :]) * SCALE
        dv = mm(low[row_at, first:], on[first:, :])
        return dk, dv

    def add_query_grads(zz, key_blocks, p):
        keys_t = jnp.concatenate([jnp.transpose(kv[2 * zz + kb, 0]) for kb in key_blocks], axis=1)
        for h in range(0, GROUP, 2):
            at = slice(p * wide + h * rows, p * wide + (h + 2) * rows)
            dqt[:, at] += mm(keys_t, scored[:len(key_blocks) * rows, at])

    def pair_step(zz):
        for kb in range(2):
            for p in range(2):
                score_grads(zz, kb, p)
            dk, dv = key_value_grads(kb, 0)
            zsend[2 * zz + kb, 0] = dk.astype(BF16)
            zsend[2 * zz + kb, 1] = dv.astype(BF16)
            pl.when(z == half - 1)(lambda b=2 * zz + kb: zgrad_copy(b).start())

        for p in range(2):
            add_query_grads(zz, (0, 1), p)
    loop(0, z, pair_step)
    next_to_last = (z == half - 2) & (z > 0)

    @pl.when(next_to_last)
    def _():
        relay(0)
        relay(1)

    y_copy(3).wait_recv()
    mine = mine + trecv[0, 0:1, :]
    tsend[1] = jnp.broadcast_to(mine, tsend.shape[1:])
    tensor_copy().start()

    for kb, p in ((0, 0), (0, 1), (1, 1)):
        score_grads(z, kb, p)
    add_query_grads(z, (0,), 0)
    add_query_grads(z, (0, 1), 1)
    for h in range(GROUP):
        dqx[:, h * D:(h + 1) * D] = jnp.transpose(dqt[:, lanes(1 - y, h)] * SCALE).astype(BF16)
    y_copy(4).start()
    for kb in range(2):
        dk, dv = key_value_grads(kb, kb * wide)
        own[kb, 0] = dk
        own[kb, 1] = dv
    for h in range(GROUP):
        dq_ref[:, head_columns(y, h)] = jnp.transpose(dqt[:, lanes(y, h)] * SCALE).astype(BF16)

    @pl.when(z < half - 1)
    def _():
        loop(jnp.where(next_to_last, 2, 0), 2 * z, relay)
        for kb in range(2):
            zgrad_copy(2 * z + kb).wait_recv()
            own[kb] = own[kb] + zrecv[2 * z + kb].astype(F32)

    dkvx[...] = own[1 - y].astype(BF16)
    y_copy(5).start()
    dk_ref[:, column(y)] = own[y, 0].astype(BF16)
    dv_ref[:, column(y)] = own[y, 1].astype(BF16)
    tensor_copy().wait_recv()
    dgate_ref[...] = (1.0 - gate) * (mine + trecv[1, 0:1, :])
    y_copy(4).wait_recv()
    dq_ref[:, pl.ds(pl.multiple_of((1 - y) * GROUP * D, GROUP * D), GROUP * D)] = dqr[...]
    y_copy(5).wait_recv()
    dk_ref[:, column(1 - y)] = dkvr[0]
    dv_ref[:, column(1 - y)] = dkvr[1]

    for i in range(6):
        y_copy(i).wait_send()
    tensor_copy().wait_send()

    @pl.when(z < half - 1)
    def _():
        loop(0, 2 * z + 2, lambda b: up_copy(b).wait_send())

    loop(0, 2 * z, lambda b: zgrad_copy(b).wait_send())


def hand_over(*refs):
    count = len(refs) // 2
    for source, target in zip(refs[:count], refs[count:]):
        target[...] = source[...]


def local(n, queries, keys, values, grad_out, gate_logit, block_ids, block_counts):
    rows, width = queries.shape
    kv_width = keys.shape[1]
    assert kv_width == 2 * D and width == 2 * GROUP * D and n % 2 == 0
    half = n // 2
    wide = GROUP * rows
    vmem = pl.BlockSpec(memory_space=pltpu.VMEM)
    smem = pl.BlockSpec(memory_space=pltpu.SMEM)
    pair = (2, rows, D)
    sem = pltpu.SemaphoreType.DMA
    row = pltpu.VMEM((1, 2 * wide), F32)
    dq, dk, dv, dgate = pl.pallas_call(
        functools.partial(kernel, n),
        out_shape=(
            jax.ShapeDtypeStruct((rows, width), BF16),
            jax.ShapeDtypeStruct((rows, kv_width), BF16),
            jax.ShapeDtypeStruct((rows, kv_width), BF16),
            jax.ShapeDtypeStruct((1, rows), F32),
        ),
        in_specs=[smem, smem, vmem, vmem, vmem, vmem, vmem],
        out_specs=(vmem, vmem, vmem, vmem),
        scratch_shapes=[
            pltpu.VMEM((n,) + pair, BF16),
            pltpu.VMEM(pair, BF16),
            pltpu.VMEM((wide, D), BF16),
            pltpu.VMEM((wide, D), BF16),
            pltpu.VMEM((2 * wide, D), BF16),
            pltpu.VMEM((D, 2 * wide), BF16),
            pltpu.VMEM((2 * wide, D), BF16),
            pltpu.VMEM((D, 2 * wide), BF16),
            pltpu.VMEM((n, rows, 2 * wide), BF16),
            pltpu.VMEM((n, 1, 2 * wide), F32),
            row, row,
            pltpu.VMEM((D, 2 * wide), F32),
            row, row,
            pltpu.VMEM((D, 2 * wide), F32),
            pltpu.VMEM((2,) + pair, F32),
            pltpu.VMEM((2, rows, rows), F32),
            pltpu.VMEM((2 * rows, 2 * wide), BF16),
            pltpu.VMEM((2 * rows, 2 * wide), BF16),
            pltpu.VMEM((n,) + pair, BF16),
            pltpu.VMEM((n,) + pair, BF16),
            pltpu.VMEM((rows, GROUP * D), BF16),
            pltpu.VMEM((rows, GROUP * D), BF16),
            pltpu.VMEM(pair, BF16),
            pltpu.VMEM(pair, BF16),
            pltpu.VMEM((2, 8, rows), F32),
            pltpu.VMEM((2, 8, rows), F32),
            sem((n,)),
            sem((n,)),
            sem((n,)),
            sem((n,)),
            sem((6,)),
            sem((6,)),
            sem((2,)),
        ],
        compiler_params=pltpu.CompilerParams(
            collective_id=0, has_side_effects=True, vmem_limit_bytes=62 * 1024 * 1024
        ),
        cost_estimate=pl.CostEstimate(
            flops=12 * n * rows * rows * width,
            bytes_accessed=6 * rows * (width + kv_width),
            transcendentals=n * rows * rows * width // D,
        ),
        name="mod_attention_grads",
    )(block_ids.T, block_counts, queries, keys, values, grad_out, gate_logit.reshape(1, rows))
    results = (dq, dk, dv, dgate)
    dq, dk, dv, dgate = pl.pallas_call(
        hand_over,
        out_shape=tuple(jax.ShapeDtypeStruct(x.shape, x.dtype) for x in results),
        in_specs=[vmem] * 4,
        out_specs=(vmem,) * 4,
        name="hand_over",
    )(*results)
    return dq, dk, dv, dgate.reshape(rows)


def solution(mesh):
    in_specs = (
        P(("dp", "seq"), "tensor"),
        P(("dp", "seq"), "tensor"),
        P(("dp", "seq"), "tensor"),
        P(("dp", "seq"), "tensor"),
        P(("dp", "seq")),
        P("dp", None),
        P("dp"),
    )
    out_specs = (
        P(("dp", "seq"), "tensor"),
        P(("dp", "seq"), "tensor"),
        P(("dp", "seq"), "tensor"),
        P(("dp", "seq")),
    )
    return jax.shard_map(
        functools.partial(local, mesh.shape["seq"]),
        mesh=mesh, in_specs=in_specs, out_specs=out_specs, check_vma=False,
    )
```
